512 devices in a mesh: peer: 32 (over y_lo, z), grp: 16 (over y_hi, x, core).
Axes of the slice: x: 4, y: 4 (y_hi: 2, y_lo: 2; y = y_hi * 2 + y_lo), z: 16, core: 2. Of those that a mesh axis runs over, the one named last changes fastest.
Arguments:
- tokens: bfloat16 [65536, 2048], P(('peer', 'grp')), may hold values from -6 to 6
- cotangent: bfloat16 [65536, 2048], P(('peer', 'grp')), may hold values from -6 to 6
- expert_ids: int32 [65536, 4], P(('peer', 'grp')), may hold values from 0 to 31, all different within a row; in each aligned block of 128 rows (0 to 127, 128 to 255, ...) at most 32 rows name the same one
- route_prob: float32 [65536, 4], P(('peer', 'grp')), may hold values from 0.1 to 1
- w_gate: bfloat16 [32, 2048, 2816], P('peer', None, 'grp'), may hold values from -0.125 to 0.125
- w_up: bfloat16 [32, 2048, 2816], P('peer', None, 'grp'), may hold values from -0.125 to 0.125
- w_down: bfloat16 [32, 2816, 2048], P('peer', 'grp'), may hold values from -0.21875 to 0.21875
- student_logits: bfloat16 [32, 8, 151936], P('peer', None, 'grp'), may hold values from -24 to 252
- stale_logits: bfloat16 [32, 8, 151936], P('peer', None, 'grp'), may hold values from -24 to 252
- labels: int32 [32, 8], P('peer'), may hold values from 0 to 151935
Outputs:
- layer_out: bfloat16 [65536, 2048], P(('peer', 'grp'))
- input_grad: bfloat16 [65536, 2048], P(('peer', 'grp'))
- prob_grad: float32 [65536, 4], P(('peer', 'grp'))
- distill_loss: float32 [32, 8], P('peer')
- logit_grad: bfloat16 [32, 8, 151936], P('peer', None, 'grp')
The draws below stay inside these ranges and needn't reach their ends.
Inputs may be any that keep to these rules, and one draw needn't show every extreme that they name: `expert_ids`: each row names 4 different experts; the rows of one device name any one expert at most 32 times.
All inputs are finite; a program needn't handle non-finite values.
Results may differ from the reference program's by a relative error of at most 0.0064.
Values may be sent and summed in bfloat16 or wider, within the bound.
A program may use at most 64 MiB of HBM per device.

```python
import math
import jax
import jax.numpy as jnp
import numpy as np
from jax import lax

D = 2048
VOCAB = 151936
TOPK = 4
EXPERTS = 32
HID = 704
PIECES = 4
TOK_DEV = 128
LROWS = 8
CAP = 32
FF_PIECE = 176
PEERS = 32
TOKENS = 65536
COLS = 2816
N_PEER = 32
N_GRP = 16


def logit_field(key, salt_value):
    key = jax.random.fold_in(key, salt_value)
    key_list = jax.random.split(key, 1)
    logit_shape = (PEERS, LROWS, VOCAB)
    scores = jnp.clip(4.0 * jax.random.normal(key_list[0], logit_shape, jnp.float32), -24.0, 24.0)
    return scores


def draw_student_logits(key, part):
    return logit_field(key, 101).astype(jnp.bfloat16)


def draw_stale_logits(key, part):
    return logit_field(key, 202).astype(jnp.bfloat16)


def plant(values, rng, smallest, top_value):
    spot = [jax.random.randint(jax.random.fold_in(rng, axis), (), 0, length) for axis, length in enumerate(values.shape)]
    longest = values.shape.index(max(values.shape))
    next_to = spot[:longest] + [(spot[longest] + 1) % values.shape[longest]] + spot[longest + 1:]
    return values.at[tuple(spot)].set(smallest).at[tuple(next_to)].set(top_value)


def steps_of(stream_key, dims, cuts, smallest, largest):
    def one(dim, shards_of):
        draws = jax.random.uniform(jax.random.fold_in(jax.random.fold_in(stream_key, 6), dim), (shards_of,), jnp.float32, smallest / len(cuts), largest / len(cuts))
        return jnp.repeat(jnp.exp(draws), dims[dim] // shards_of).reshape((-1,) + (1,) * (len(dims) - dim - 1))

    loudness = one(*cuts[0])
    for cut in cuts[1:]:
        loudness = loudness * one(*cut)
    return loudness


def routed_block(stream_key, own, number, rows, count, top, limit, lean):
    ranking = jax.random.permutation(stream_key, count)
    crowded, common = shares(count, rows * top, limit, lean, True), shares(count, rows * top, limit, lean, False)
    places = jnp.arange(count)

    def named(sizes, rotation):
        used = int((sizes > 0).sum())
        fixed = max(1, used // 4)
        passed = fixed + (places - fixed + rotation * (used - fixed)) % max(1, count - fixed)
        return jnp.zeros((count,), jnp.int32).at[ranking[jnp.where(places < fixed, places, passed)]].set(jnp.asarray(sizes, jnp.int32))

    sizes = jnp.where(number % 4 == 0, named(crowded, number // 4), named(common, number - number // 4 - 1))
    mixed = jax.random.permutation(jax.random.fold_in(own, 3), count)
    giver, taker = mixed[0:count // 2 * 2:2], mixed[1:count // 2 * 2:2]
    room = jnp.minimum(sizes[giver] - 1, limit - sizes[taker]) // 2
    room = jnp.where((giver == ranking[0]) | (taker == ranking[0]) | (sizes[taker] == 0), 0, jnp.maximum(room, 0))
    passed = jax.random.randint(jax.random.fold_in(own, 4), (count // 2,), 0, 1 << 20) % (room + 1)
    sizes = sizes.at[giver].add(-passed).at[taker].add(passed)
    members = jnp.searchsorted(jnp.cumsum(sizes), jnp.arange(rows * top), side="right").astype(jnp.int32)
    grid = members.reshape(top, rows).T
    grid = grid[jax.random.permutation(jax.random.fold_in(own, 1), rows)]
    rotation = jax.random.randint(jax.random.fold_in(own, 2), (rows, 1), 0, top)
    return jnp.take_along_axis(grid, (jnp.arange(top)[None, :] + rotation) % top, axis=1)


def shares(count, total, reach, skew, full):
    loads = [(1 << 20) // math.isqrt(grade ** skew) + 1 for grade in range(1, count + 1)]
    largest = reach if full else min(reach, max(-(-total // count), total * loads[0] // sum(loads)))
    least = 1 if total - largest >= count - 1 else 0
    given, rest = [largest] + [least] * (count - 1), total - largest - least * (count - 1)
    while rest > 0:
        free = [i for i in range(1, count) if given[i] < largest] or [i for i in range(1, count) if given[i] < reach]
        whole, remaining = sum([loads[i] for i in free]), rest
        for i in free:
            more = min(reach - given[i], max(1, remaining * loads[i] // whole), rest)
            given[i] = given[i] + more
            rest = rest - more
    return np.array(given)


def noise(rng, shape, scale, most, shards=(), kind=jnp.bfloat16):
    values = scale * jax.random.normal(rng, shape, jnp.float32)
    if shards:
        values = values * steps_of(rng, shape, shards, -0.22, 0.18)
    return jnp.clip(values, -most, most).astype(kind)


def setup_inputs(seed: int = 0) -> dict:
    streams_of = jax.random.split(jax.random.key(seed), 11)
    tokens = noise(streams_of[0], (TOKENS, D), 1.0, 6.0, ((0, 512),))
    cotangent = noise(streams_of[1], (TOKENS, D), 1.0, 6.0, ((0, 512),))
    expert_ids_keys = jax.random.split(jax.random.fold_in(streams_of[2], 1), TOKENS // TOK_DEV)
    expert_ids_turns = jax.random.permutation(jax.random.fold_in(streams_of[2], 3), TOKENS // TOK_DEV)
    expert_ids = jax.vmap(lambda own, number: routed_block(jax.random.fold_in(streams_of[2], 2), own, number, TOK_DEV, EXPERTS, TOPK, CAP, 2))(expert_ids_keys, expert_ids_turns).reshape((TOKENS, TOPK))
    route_prob = jnp.clip(0.1 + 0.9 * jax.random.uniform(streams_of[3], (TOKENS, TOPK), jnp.float32) ** steps_of(streams_of[3], (TOKENS, TOPK), ((0, 512),), -0.2, 0.2), 0.1, 1.0)
    w_gate = noise(streams_of[4], (PEERS, D, COLS), D ** -0.5, 0.125, ((0, 32), (2, 16)))
    w_up = noise(streams_of[5], (PEERS, D, COLS), D ** -0.5, 0.125, ((0, 32), (2, 16)))
    w_down = noise(streams_of[6], (PEERS, COLS, D), HID ** -0.5, 0.21875, ((0, 32), (1, 16)))
    student_logits = draw_student_logits(jax.random.fold_in(streams_of[10], 71), 0)
    stale_logits = draw_stale_logits(jax.random.fold_in(streams_of[10], 71), 0)
    labels = plant(jax.random.randint(streams_of[9], (PEERS, LROWS), 0, VOCAB), jax.random.fold_in(streams_of[9], 1), 0, VOCAB - 1).astype(jnp.int32)
    return {"tokens": tokens, "cotangent": cotangent, "expert_ids": expert_ids, "route_prob": route_prob, "w_gate": w_gate, "w_up": w_up, "w_down": w_down, "student_logits": student_logits, "stale_logits": stale_logits, "labels": labels}


def slot_tables(expert_ids, n_window, capacity):
    window_iota = lax.broadcasted_iota(jnp.int32, (1, 1, n_window), 2)
    member = jnp.sum((expert_ids[:, :, None] == window_iota).astype(jnp.int32), axis=1).astype(jnp.int32)
    position = (jnp.cumsum(member, axis=0) - member).astype(jnp.int32)
    slot_iota = lax.broadcasted_iota(jnp.int32, (1, capacity, 1), 1)
    select = (position.T[:, None, :] == slot_iota) & (member.T[:, None, :] > 0)
    return position, select


def forward_piece(slot_rows, gate_cols, up_cols, down_rows):
    gate_act = jnp.dot(slot_rows, gate_cols, preferred_element_type=jnp.float32)
    up_act = jnp.dot(slot_rows, up_cols, preferred_element_type=jnp.float32)
    hidden = (gate_act * jax.nn.sigmoid(gate_act) * up_act).astype(jnp.bfloat16)
    piece_out = jnp.dot(hidden, down_rows, preferred_element_type=jnp.float32).astype(jnp.bfloat16)
    return piece_out, gate_act, up_act


def backward_piece(scaled_rows, gate_act, up_act, gate_cols, up_cols, down_rows):
    contract = (((1,), (1,)), ((), ()))
    grad_hidden = lax.dot_general(scaled_rows, down_rows, contract, preferred_element_type=jnp.float32)
    sigmoid_gate = jax.nn.sigmoid(gate_act)
    grad_gate = (grad_hidden * up_act * sigmoid_gate * (1.0 + gate_act * (1.0 - sigmoid_gate))).astype(jnp.bfloat16)
    grad_up = (grad_hidden * gate_act * sigmoid_gate).astype(jnp.bfloat16)
    piece_grad = lax.dot_general(grad_gate, gate_cols, contract, preferred_element_type=jnp.float32)
    piece_grad = piece_grad + lax.dot_general(grad_up, up_cols, contract, preferred_element_type=jnp.float32)
    return piece_grad.astype(jnp.bfloat16)


def reference(tokens, cotangent, expert_ids, route_prob, w_gate, w_up, w_down, student_logits, stale_logits, labels):
    n_window = N_GRP // PIECES
    tok_blocks = tokens.reshape(N_PEER, N_GRP, TOK_DEV, D)
    cot_blocks = cotangent.reshape(N_PEER, N_GRP, TOK_DEV, D)
    id_blocks = expert_ids.reshape(N_PEER, N_GRP, TOK_DEV, TOPK)
    prob_blocks = route_prob.reshape(N_PEER, N_GRP, TOK_DEV, TOPK)

    def prepare(src_tokens, src_cot, src_ids, src_prob):
        position, select = slot_tables(src_ids, n_window, CAP)
        select_f = select.astype(jnp.float32)
        window_iota = lax.broadcasted_iota(jnp.int32, (1, 1, n_window), 2)
        token_prob = jnp.sum(src_prob[:, :, None] * (src_ids[:, :, None] == window_iota).astype(jnp.float32), axis=1)
        slot_prob = jnp.einsum("ect,te->ec", select_f, token_prob, precision=lax.Precision.HIGHEST)
        slot_rows = jnp.einsum("ect,td->ecd", select_f, src_tokens.astype(jnp.float32), precision=lax.Precision.HIGHEST).astype(jnp.bfloat16)
        slot_cot = jnp.einsum("ect,td->ecd", select_f, src_cot.astype(jnp.float32), precision=lax.Precision.HIGHEST)
        slot_scaled = (slot_prob[:, :, None] * slot_cot).astype(jnp.bfloat16)
        return slot_rows, slot_scaled, position

    def combine(expert_out, expert_grad, src_ids, src_prob, src_cot, position):
        in_window = src_ids < n_window
        safe_ids = jnp.where(in_window, src_ids, 0).astype(jnp.int32)
        slot_index = jnp.take_along_axis(position, safe_ids, axis=1).astype(jnp.int32)
        flat_index = (safe_ids * CAP + slot_index).astype(jnp.int32)
        out_rows = jnp.where(in_window[:, :, None], jnp.take(expert_out.reshape(-1, D), flat_index, axis=0), 0.0)
        grad_rows = jnp.where(in_window[:, :, None], jnp.take(expert_grad.reshape(-1, D), flat_index, axis=0), 0.0)
        layer_out = jnp.sum(src_prob[:, :, None] * out_rows, axis=1).astype(jnp.bfloat16)
        prob_grad = jnp.sum(src_cot.astype(jnp.float32)[:, None, :] * out_rows, axis=2)
        input_grad = jnp.sum(grad_rows, axis=1).astype(jnp.bfloat16)
        return layer_out, input_grad, prob_grad

    def one_peer(packed):
        peer_tokens, peer_cot, peer_ids, peer_prob, gate_cols, up_cols, down_rows = packed
        slot_rows, slot_scaled, position = jax.vmap(prepare)(peer_tokens, peer_cot, peer_ids, peer_prob)

        def one_piece(piece):
            expert = piece // PIECES
            rows_in = lax.dynamic_index_in_dim(slot_rows, expert, 1, keepdims=False).reshape(-1, D)
            scaled_in = lax.dynamic_index_in_dim(slot_scaled, expert, 1, keepdims=False).reshape(-1, D)
            start = (piece * FF_PIECE).astype(jnp.int32)
            gate_piece = lax.dynamic_slice_in_dim(gate_cols, start, FF_PIECE, 1)
            up_piece = lax.dynamic_slice_in_dim(up_cols, start, FF_PIECE, 1)
            down_piece = lax.dynamic_slice_in_dim(down_rows, start, FF_PIECE, 0)
            piece_out, gate_act, up_act = forward_piece(rows_in, gate_piece, up_piece, down_piece)
            piece_grad = backward_piece(scaled_in, gate_act, up_act, gate_piece, up_piece, down_piece)
            return piece_out, piece_grad

        piece_out, piece_grad = lax.map(one_piece, jnp.arange(N_GRP, dtype=jnp.int32))
        expert_out = jnp.sum(piece_out.astype(jnp.float32).reshape(n_window, PIECES, N_GRP, CAP, D), axis=1)
        expert_grad = jnp.sum(piece_grad.astype(jnp.float32).reshape(n_window, PIECES, N_GRP, CAP, D), axis=1)
        expert_out = jnp.transpose(expert_out, (1, 0, 2, 3))
        expert_grad = jnp.transpose(expert_grad, (1, 0, 2, 3))
        return jax.vmap(combine)(expert_out, expert_grad, peer_ids, peer_prob, peer_cot, position)

    layer_out, input_grad, prob_grad = lax.map(one_peer, (tok_blocks, cot_blocks, id_blocks, prob_blocks, w_gate, w_up, w_down))
    layer_out = layer_out.reshape(TOKENS, D)
    input_grad = input_grad.reshape(TOKENS, D)
    prob_grad = prob_grad.reshape(TOKENS, TOPK)

    student = student_logits.astype(jnp.float32)
    teacher = jnp.roll(stale_logits, 1, axis=0).astype(jnp.float32)
    max_student = jnp.max(student, axis=2, keepdims=True)
    lse_student = max_student + jnp.log(jnp.sum(jnp.exp(student - max_student), axis=2, keepdims=True))
    max_teacher = jnp.max(teacher, axis=2, keepdims=True)
    lse_teacher = max_teacher + jnp.log(jnp.sum(jnp.exp(teacher - max_teacher), axis=2, keepdims=True))
    teacher_prob = jnp.exp(teacher - lse_teacher)
    vocab_iota = lax.broadcasted_iota(jnp.int32, student.shape, 2)
    label_hit = vocab_iota == labels[:, :, None]
    label_logit = jnp.sum(jnp.where(label_hit, student, 0.0), axis=2)
    cross_term = jnp.sum(teacher_prob * (teacher - student), axis=2)
    distill_loss = 2.0 * lse_student[:, :, 0] - label_logit + cross_term - lse_teacher[:, :, 0]
    logit_grad = (2.0 * jnp.exp(student - lse_student) - label_hit.astype(jnp.float32) - teacher_prob).astype(jnp.bfloat16)
    return layer_out, input_grad, prob_grad, distill_loss, logit_grad
```

```python
import functools

import jax
import jax.numpy as jnp
from jax import lax
from jax.experimental import pallas as pl
from jax.experimental.pallas import tpu as pltpu
from jax.sharding import PartitionSpec as P

MESH = pl.DeviceIdType.MESH
CAP = 32
CHIPS = 8
BATCHES = ((0,), (6,), (1, 7), (3, 5), (4, 2))
ORDER = tuple(r for batch in BATCHES for r in batch)
F32 = jnp.float32
BF16 = jnp.bfloat16
NT = (((1,), (1,)), ((), ()))


def dot(a, b):
    return jnp.dot(a, b, preferred_element_type=F32)


def dot_nt(a, b):
    return lax.dot_general(a, b, NT, preferred_element_type=F32)


def kernel(
    tok_h, cot_h, ids_h, prob_h, wg_h, wu_h, wd_h, stu_h, sta_h, lab_h,
    lay_h, ing_h, pgr_h, loss_h, lgr_h,
    tok, cot, ids, prob, wg, wu, wd, stu, tea, lab,
    lay, ing, pgr, loss, lgr,
    send, take, part, back, stat, in_sem, out_sem, far_send, far_recv, w_send, w_recv,
    d_send, d_recv, r_send, r_recv, s_send, s_recv, t_send, t_recv,
):
    peer, grp = lax.axis_index("peer"), lax.axis_index("grp")
    n_peer, n_grp = lax.axis_size("peer"), lax.axis_size("grp")
    chip, core = grp // 2, grp % 2
    twin = (peer, chip * 2 + (1 - core))
    after = (lax.rem(peer + 1, n_peer), grp)
    before = (lax.rem(peer + n_peer - 1, n_peer), grp)

    def xor(a, bits, width):
        out = a
        for b in range(width):
            if bits >> b & 1:
                out = out + (1 << b) * (1 - 2 * ((a // (1 << b)) % 2))
        return out

    def chip_at(r):
        return (peer, xor(chip, r, 3) * 2 + core)

    def member_at(k):
        return (peer, xor(grp, k, 4))

    barrier = pltpu.get_barrier_semaphore()
    for k in range(1, 16):
        pl.semaphore_signal(barrier, inc=1, device_id=member_at(k), device_id_type=MESH)
    pl.semaphore_signal(barrier, inc=1, device_id=after, device_id_type=MESH)
    pl.semaphore_signal(barrier, inc=1, device_id=before, device_id_type=MESH)

    loads = [
        pltpu.make_async_copy(src, dst, in_sem.at[i])
        for i, (src, dst) in enumerate(
            (
                (ids_h, ids), (prob_h, prob), (tok_h, tok), (cot_h, cot), (stu_h.at[0], stu), (lab_h, lab),
                (wg_h.at[0], wg), (wu_h.at[0], wu), (wd_h.at[0], wd),
            )
        )
    ]
    for copy in loads:
        copy.start()

    loads[0].wait()
    loads[1].wait()
    lanes = lax.broadcasted_iota(jnp.int32, (1, CHIPS * CAP), 1)
    own_expert = chip // 2
    lane_pair = lanes // (2 * CAP)
    lane_expert = (own_expert // 2 + lane_pair // 2) % 2 * 2 + (own_expert + lane_pair) % 2
    lane_slot = lanes % CAP
    hits = [ids[:, k : k + 1] == lane_expert for k in range(4)]
    member = functools.reduce(jnp.add, [h.astype(F32) for h in hits])
    rows = lax.broadcasted_iota(jnp.int32, (128, 128), 0)
    columns = lax.broadcasted_iota(jnp.int32, (128, 128), 1)
    earlier = (columns < rows).astype(F32).astype(BF16)
    position = dot(earlier, member.astype(BF16))
    chosen = jnp.where((member > 0.0) & (position.astype(jnp.int32) == lane_slot), 1.0, 0.0)
    weight = functools.reduce(
        jnp.add, [jnp.where(h, prob[:, k : k + 1], 0.0) for k, h in enumerate(hits)]
    ) * chosen
    picks = []
    for j in range(4):
        picks.append(slice(j * 2 * CAP, j * 2 * CAP + CAP))
    chosen_4 = jnp.concatenate([chosen[:, p] for p in picks], axis=1)
    weight_4 = jnp.concatenate([weight[:, p] for p in picks], axis=1)
    gather = chosen_4.T.astype(BF16)
    slot_prob = jnp.sum(weight_4.T, axis=1, keepdims=True)
    loads[2].wait()
    for n in range(0, 2048, 512):
        send[0, :, :, n : n + 512] = dot(gather, tok[:, n : n + 512]).astype(BF16).reshape(4, CAP, 512)
    loads[3].wait()
    for n in range(0, 2048, 512):
        send[1, :, :, n : n + 512] = (
            (slot_prob * dot(gather, cot[:, n : n + 512])).astype(BF16).reshape(4, CAP, 512)
        )

    pl.semaphore_wait(barrier, 17)

    def remote(src, dst, s, r, target):
        return pltpu.make_async_remote_copy(
            src_ref=src, dst_ref=dst, send_sem=s, recv_sem=r, device_id=target, device_id_type=MESH
        )

    spot = {r: i for i, r in enumerate(ORDER)}
    out_going = {
        r: remote(send.at[:, r // 2], take.at[:, spot[r]], d_send.at[r], d_recv.at[r], chip_at(r))
        for r in ORDER
        if r
    }
    returning = {
        r: remote(part.at[:, spot[r]], back.at[:, r], r_send.at[r], r_recv.at[r], chip_at(r))
        for r in ORDER
        if r
    }
    swaps = [
        remote(src, dst, w_send.at[i], w_recv.at[i], twin)
        for i, (src, dst) in enumerate(
            ((wg_h.at[0], far_send.at[0]), (wu_h.at[0], far_send.at[1]), (wd_h.at[0], far_recv))
        )
    ]
    teacher_copy = remote(sta_h.at[0], tea, t_send, t_recv, after)
    for r in ORDER:
        if r:
            out_going[r].start()
    for copy in swaps:
        copy.start()
    teacher_copy.start()

    take[:, 0] = send[:, 0]

    loads[4].wait()
    loads[5].wait()
    teacher_copy.wait_recv()
    eye = lax.broadcasted_iota(jnp.int32, (8, 8), 0) == lax.broadcasted_iota(jnp.int32, (8, 8), 1)
    label = jnp.sum(jnp.where(eye, lab[...].astype(F32), 0.0), axis=1, keepdims=True).astype(jnp.int32)
    student = stu[...].astype(F32)
    teacher = tea[...].astype(F32)
    width = student.shape[1]
    vocab = grp * width + lax.broadcasted_iota(jnp.int32, student.shape, 1)
    lane = lax.broadcasted_iota(jnp.int32, (8, 128), 1)
    top_s = jnp.max(student, axis=1, keepdims=True)
    top_t = jnp.max(teacher, axis=1, keepdims=True)
    exp_t = jnp.exp(teacher - top_t)
    stats = (
        top_s,
        top_t,
        jnp.sum(jnp.exp(student - top_s), axis=1, keepdims=True),
        jnp.sum(exp_t, axis=1, keepdims=True),
        jnp.sum(exp_t * (teacher - student), axis=1, keepdims=True),
        jnp.sum(jnp.where(vocab == label, student, 0.0), axis=1, keepdims=True),
    )
    stat[0] = functools.reduce(
        jnp.add, [jnp.where(lane == i, s, 0.0) for i, s in enumerate(stats)]
    )
    telling = [
        remote(stat.at[0], stat.at[k], s_send.at[k], s_recv.at[k], member_at(k)) for k in range(1, 16)
    ]
    for copy in telling:
        copy.start()

    for copy in loads[6:]:
        copy.wait()
    for copy in swaps:
        copy.wait()
    halves = ((wg, wu, wd), (far_send.at[0], far_send.at[1], far_recv))
    for batch in BATCHES:
        for r in batch:
            if r:
                out_going[r].wait_recv()
        first, count = spot[batch[0]], len(batch)
        x = take[0, first : first + count].reshape(count * CAP, 2048)
        s = take[1, first : first + count].reshape(count * CAP, 2048)
        inner = []
        for gate_w, up_w, down_w in halves:
            gate = dot(x, gate_w[...])
            up = dot(x, up_w[...])
            grad = dot_nt(s, down_w[...])
            sig = jax.nn.sigmoid(gate)
            hidden = (gate * sig * up).astype(BF16)
            grad_gate = (grad * up * sig * (1.0 + gate * (1.0 - sig))).astype(BF16)
            grad_up = (grad * gate * sig).astype(BF16)
            inner.append((hidden, grad_gate, grad_up))
        for n in range(0, 2048, 512):
            cut = slice(n, n + 512)
            out_piece = functools.reduce(
                jnp.add, [dot(i[0], h[2][:, cut]) for i, h in zip(inner, halves)]
            )
            grad_piece = functools.reduce(
                jnp.add,
                [dot_nt(i[1], h[0][cut, :]) + dot_nt(i[2], h[1][cut, :]) for i, h in zip(inner, halves)],
            )
            for kind, value in ((0, out_piece), (1, grad_piece)):
                value = value.astype(BF16).reshape(count, CAP, 512)
                if batch == (0,):
                    back[kind, 0, :, cut] = value[0]
                else:
                    part[kind, first : first + count, :, cut] = value
        for r in batch:
            if r:
                returning[r].start()

    for copy in telling:
        copy.wait()
    seen = [stat[k] for k in range(16)]
    def col(k, i):
        return seen[k][:, i : i + 1]
    max_s = functools.reduce(jnp.maximum, [col(k, 0) for k in range(16)])
    max_t = functools.reduce(jnp.maximum, [col(k, 1) for k in range(16)])
    scale_s = [jnp.exp(col(k, 0) - max_s) for k in range(16)]
    scale_t = [jnp.exp(col(k, 1) - max_t) for k in range(16)]
    sum_s = functools.reduce(jnp.add, [col(k, 2) * scale_s[k] for k in range(16)])
    sum_t = functools.reduce(jnp.add, [col(k, 3) * scale_t[k] for k in range(16)])
    cross = functools.reduce(jnp.add, [col(k, 4) * scale_t[k] for k in range(16)])
    label_logit = functools.reduce(jnp.add, [col(k, 5) for k in range(16)])
    lse_s = max_s + jnp.log(sum_s)
    lse_t = max_t + jnp.log(sum_t)
    value = 2.0 * lse_s - label_logit + cross / sum_t - lse_t
    loss[...] = jnp.sum(jnp.where(eye, value, 0.0), axis=0, keepdims=True)
    student = stu[...].astype(F32)
    teacher = tea[...].astype(F32)
    onehot = jnp.where(vocab == label, 1.0, 0.0)
    lgr[...] = (2.0 * jnp.exp(student - lse_s) - onehot - jnp.exp(teacher - lse_t)).astype(BF16)

    for r in ORDER:
        if r:
            returning[r].wait_recv()
    weight_hi = weight.astype(BF16)
    weight_lo = (weight - weight_hi.astype(F32)).astype(BF16)
    chosen_bf = chosen.astype(BF16)
    out_rows = back[0].reshape(CHIPS * CAP, 2048)
    inner_product = dot_nt(cot[...], out_rows) * chosen
    lane4 = lax.broadcasted_iota(jnp.int32, (128, 4), 1)
    pgr[...] = functools.reduce(
        jnp.add,
        [
            jnp.where(lane4 == k, jnp.sum(jnp.where(h, inner_product, 0.0), axis=1, keepdims=True), 0.0)
            for k, h in enumerate(hits)
        ],
    )
    for n in range(0, 2048, 512):
        cut = slice(n, n + 512)
        rows_n = back[0, :, :, cut].reshape(CHIPS * CAP, 512)
        lay[:, cut] = (dot(weight_hi, rows_n) + dot(weight_lo, rows_n)).astype(BF16)
        ing[:, cut] = dot(chosen_bf, back[1, :, :, cut].reshape(CHIPS * CAP, 512)).astype(BF16)
    stores = [
        pltpu.make_async_copy(src, dst, out_sem.at[i])
        for i, (src, dst) in enumerate(
            ((lay, lay_h), (ing, ing_h), (pgr, pgr_h), (loss, loss_h), (lgr, lgr_h.at[0]))
        )
    ]
    for copy in stores:
        copy.start()
    teacher_copy.wait_send()
    for r in ORDER:
        if r:
            out_going[r].wait_send()
            returning[r].wait_send()
    for copy in stores:
        copy.wait()


def body(*args):
    tokens, cotangent, expert_ids, route_prob, w_gate, w_up, w_down, student, stale, labels = args
    width = student.shape[2]
    dma = pltpu.SemaphoreType.DMA
    return pl.pallas_call(
        kernel,
        name="layer",
        out_shape=(
            jax.ShapeDtypeStruct(tokens.shape, BF16),
            jax.ShapeDtypeStruct(tokens.shape, BF16),
            jax.ShapeDtypeStruct(route_prob.shape, F32),
            jax.ShapeDtypeStruct(labels.shape, F32),
            jax.ShapeDtypeStruct(student.shape, BF16),
        ),
        in_specs=[pl.BlockSpec(memory_space=pl.ANY)] * 10,
        out_specs=[pl.BlockSpec(memory_space=pl.ANY)] * 5,
        scratch_shapes=[
            pltpu.VMEM(tokens.shape, BF16),
            pltpu.VMEM(tokens.shape, BF16),
            pltpu.VMEM(expert_ids.shape, jnp.int32),
            pltpu.VMEM(route_prob.shape, F32),
            pltpu.VMEM(w_gate.shape[1:], BF16),
            pltpu.VMEM(w_up.shape[1:], BF16),
            pltpu.VMEM(w_down.shape[1:], BF16),
            pltpu.VMEM((8, width), BF16),
            pltpu.VMEM((8, width), BF16),
            pltpu.VMEM(labels.shape, jnp.int32),
            pltpu.VMEM(tokens.shape, BF16),
            pltpu.VMEM(tokens.shape, BF16),
            pltpu.VMEM(route_prob.shape, F32),
            pltpu.VMEM(labels.shape, F32),
            pltpu.VMEM((8, width), BF16),
            pltpu.VMEM((2, 4, CAP, 2048), BF16),
            pltpu.VMEM((2, CHIPS, CAP, 2048), BF16),
            pltpu.VMEM((2, CHIPS, CAP, 2048), BF16),
            pltpu.VMEM((2, CHIPS, CAP, 2048), BF16),
            pltpu.VMEM((16, 8, 128), F32),
            dma((9,)),
            dma((5,)),
            pltpu.VMEM((2,) + w_gate.shape[1:], BF16),
            pltpu.VMEM(w_down.shape[1:], BF16),
            dma((3,)),
            dma((3,)),
            dma((8,)),
            dma((8,)),
            dma((8,)),
            dma((8,)),
            dma((16,)),
            dma((16,)),
            dma,
            dma,
        ],
        compiler_params=pltpu.CompilerParams(
            collective_id=0, has_side_effects=True, vmem_limit_bytes=56 << 20
        ),
    )(*args)


def solution(mesh):
    rows = P(("peer", "grp"), None)
    vocab = P("peer", None, "grp")
    peer_row = P("peer", None)
    return jax.shard_map(
        body,
        mesh=mesh,
        in_specs=(
            rows, rows, rows, rows, vocab, vocab, P("peer", "grp", None), vocab, vocab, peer_row,
        ),
        out_specs=(rows, rows, rows, peer_row, vocab),
        check_vma=False,
    )
```

```python
import functools

import jax
import jax.numpy as jnp
from jax import lax
from jax.experimental import pallas as pl
from jax.experimental.pallas import tpu as pltpu
from jax.sharding import PartitionSpec as P

MESH = pl.DeviceIdType.MESH
CAP = 32
CHIPS = 8
BATCHES = ((0,), (6,), (2, 4), (5, 3), (7, 1))
ORDER = tuple(r for batch in BATCHES for r in batch)
FAR = ORDER[1:]
SPOT = {r: i for i, r in enumerate(ORDER)}
SWAP_AT = 1
TELL_AT = 3
STEP = 512
F32 = jnp.float32
BF16 = jnp.bfloat16
NT = (((1,), (1,)), ((), ()))


def dot(a, b):
    return jnp.dot(a, b, preferred_element_type=F32)


def dot_nt(a, b):
    return lax.dot_general(a, b, NT, preferred_element_type=F32)


def total(terms):
    return functools.reduce(jnp.add, terms)


def xor(a, bits, width):
    out = a
    for b in range(width):
        if bits >> b & 1:
            out = out + (1 << b) * (1 - 2 * ((a // (1 << b)) % 2))
    return out


def slot_tables(ids, prob, chip):
    rows = lax.broadcasted_iota(jnp.int32, (CHIPS * CAP, 128), 0)
    row_spot = rows // CAP
    row_expert = total(
        [jnp.where(row_spot == i, xor(chip // 2, r // 2, 2), 0) for i, r in enumerate(ORDER)]
    )
    hits = [ids[k : k + 1, :] == row_expert for k in range(4)]
    member = total([h.astype(F32) for h in hits])
    earlier = (
        lax.broadcasted_iota(jnp.int32, (128, 128), 0) < lax.broadcasted_iota(jnp.int32, (128, 128), 1)
    )
    position = dot(member.astype(BF16), earlier.astype(F32).astype(BF16))
    chosen = jnp.where((member > 0.0) & (position.astype(jnp.int32) == rows % CAP), 1.0, 0.0)
    weight = total([jnp.where(h, prob[k : k + 1, :], 0.0) for k, h in enumerate(hits)]) * chosen
    return hits, chosen, weight


def logit_views(lab, width, grp):
    eye = lax.broadcasted_iota(jnp.int32, (8, 8), 0) == lax.broadcasted_iota(jnp.int32, (8, 8), 1)
    label = jnp.sum(jnp.where(eye, lab[...].astype(F32), 0.0), axis=1, keepdims=True).astype(jnp.int32)
    vocab = grp * width + lax.broadcasted_iota(jnp.int32, (8, width), 1)
    return eye, vocab == label


def expert_kernel(
    tok_h, cot_h, ids_h, prob_h, wg_h, wu_h, wd_h, stu_h, sta_h, lab_h,
    back_h, stat_h, tea_h,
    tok, cot, ids, prob, wg, wu, wd, stu, tea, lab, send, take, part, stat, twin_w, twin_d,
    in_sem, out_sem, w_send, w_recv, d_send, d_recv, r_send, r_recv, s_send, s_recv, t_send, t_recv,
):
    peer, grp = lax.axis_index("peer"), lax.axis_index("grp")
    n_peer = lax.axis_size("peer")
    chip, core = grp // 2, grp % 2
    twin = (peer, chip * 2 + (1 - core))
    depth = n_peer // 2
    half, z = peer // depth, lax.rem(peer, depth)
    after = (half * depth + lax.rem(z + 1, depth), grp)
    before = (half * depth + lax.rem(z + depth - 1, depth), grp)
    across = ((1 - half) * depth + z, grp)

    def chip_at(r):
        return (peer, xor(chip, r, 3) * 2 + core)

    def member_at(k):
        return (peer, xor(grp, k, 4))

    barrier = pltpu.get_barrier_semaphore()
    for k in range(1, 16):
        pl.semaphore_signal(barrier, inc=1, device_id=member_at(k), device_id_type=MESH)
    for near in (after, before, across):
        pl.semaphore_signal(barrier, inc=1, device_id=near, device_id_type=MESH)

    loads = [
        pltpu.make_async_copy(src, dst, in_sem.at[i])
        for i, (src, dst) in enumerate(
            (
                (ids_h, ids), (prob_h, prob), (tok_h, tok), (cot_h, cot), (stu_h.at[0], stu), (lab_h, lab),
                (wg_h.at[0], wg), (wu_h.at[0], wu), (wd_h.at[0], wd),
            )
        )
    ]
    for copy in loads:
        copy.start()

    def remote(src, dst, s, r, target):
        return pltpu.make_async_remote_copy(
            src_ref=src, dst_ref=dst, send_sem=s, recv_sem=r, device_id=target, device_id_type=MESH
        )

    out_going = {
        (kind, r): remote(
            send.at[kind, r // 2], take.at[kind, SPOT[r]], d_send.at[kind, r], d_recv.at[kind, r], chip_at(r)
        )
        for r in FAR
        for kind in (0, 1)
    }
    returning = {
        r: remote(part.at[:, SPOT[r]], back_h.at[:, SPOT[r]], r_send.at[r], r_recv.at[r], chip_at(r))
        for r in FAR
    }
    swaps = [
        remote(src, dst, w_send.at[i], w_recv.at[i], twin)
        for i, (src, dst) in enumerate(
            ((wg_h.at[0], twin_w.at[0]), (wu_h.at[0], twin_w.at[1]), (wd_h.at[0], twin_d))
        )
    ]
    teacher_copy = remote(sta_h.at[0], tea.at[0], t_send.at[0], t_recv.at[0], after)
    teacher_swap = remote(tea.at[0], tea.at[1], t_send.at[1], t_recv.at[1], across)

    loads[0].wait()
    loads[1].wait()
    hits, chosen, weight = slot_tables(ids, prob, chip)

    def of_experts(table):
        return jnp.concatenate([table[SPOT[r] * CAP : SPOT[r] * CAP + CAP] for r in (0, 2, 4, 6)], axis=0)

    gather = of_experts(chosen).astype(BF16)
    slot_prob = jnp.sum(of_experts(weight), axis=1, keepdims=True)
    loads[2].wait()
    for n in range(0, 2048, STEP):
        cut = slice(n, n + STEP)
        send[0, :, :, cut] = dot(gather, tok[:, cut]).astype(BF16).reshape(4, CAP, STEP)
    pl.semaphore_wait(barrier, 18)
    teacher_copy.start()
    first_class = FAR[0]
    out_going[0, first_class].start()
    loads[3].wait()
    for n in range(0, 2048, STEP):
        cut = slice(n, n + STEP)
        send[1, :, :, cut] = (slot_prob * dot(gather, cot[:, cut])).astype(BF16).reshape(4, CAP, STEP)
    out_going[1, first_class].start()
    for batch in BATCHES[2:]:
        for kind in (0, 1):
            for r in batch:
                out_going[kind, r].start()
    for copy in swaps:
        copy.start()

    take[:, 0] = send[:, 0]

    mine = (z == 0).astype(jnp.int32)

    def swap_teachers():
        teacher_copy.wait_recv()

        @pl.when(z == 0)
        def _():
            teacher_swap.start()

    teacher_out = pltpu.make_async_copy(tea.at[mine], tea_h, out_sem.at[1])

    def tell():
        loads[4].wait()
        loads[5].wait()

        @pl.when(z == 0)
        def _():
            teacher_swap.wait()

        teacher_out.start()
        student = stu[...].astype(F32)
        teacher = tea[mine].astype(F32)
        eye, label_hit = logit_views(lab, student.shape[1], grp)
        lane = lax.broadcasted_iota(jnp.int32, (8, 128), 1)
        top_s = jnp.max(student, axis=1, keepdims=True)
        top_t = jnp.max(teacher, axis=1, keepdims=True)
        exp_t = jnp.exp(teacher - top_t)
        stats = (
            top_s,
            top_t,
            jnp.sum(jnp.exp(student - top_s), axis=1, keepdims=True),
            jnp.sum(exp_t, axis=1, keepdims=True),
            jnp.sum(exp_t * (teacher - student), axis=1, keepdims=True),
            jnp.sum(jnp.where(label_hit, student, 0.0), axis=1, keepdims=True),
        )
        stat[...] = total([jnp.where(lane == i, s, 0.0) for i, s in enumerate(stats)])
        stat_own.start()
        for copy in telling:
            copy.start()

    stat_own = pltpu.make_async_copy(stat, stat_h.at[0], out_sem.at[2])
    telling = [
        remote(stat, stat_h.at[k], s_send.at[k], s_recv.at[k], member_at(k)) for k in range(1, 16)
    ]
    back_own = pltpu.make_async_copy(part.at[:, 0], back_h.at[:, 0], out_sem.at[0])

    for copy in loads[6:]:
        copy.wait()
    for copy in swaps:
        copy.wait()
    halves = ((wg, wu, wd), (twin_w.at[0], twin_w.at[1], twin_d))
    for step, batch in enumerate(BATCHES):
        for r in batch:
            if r:
                out_going[0, r].wait_recv()
                out_going[1, r].wait_recv()
        first, count = SPOT[batch[0]], len(batch)
        x = take[0, first : first + count].reshape(count * CAP, 2048)
        s = take[1, first : first + count].reshape(count * CAP, 2048)
        inner = []
        for gate_w, up_w, down_w in halves:
            gate = dot_nt(x, gate_w[...])
            up = dot_nt(x, up_w[...])
            grad = dot_nt(s, down_w[...])
            sig = jax.nn.sigmoid(gate)
            hidden = (gate * sig * up).astype(BF16)
            grad_gate = (grad * up * sig * (1.0 + gate * (1.0 - sig))).astype(BF16)
            grad_up = (grad * gate * sig).astype(BF16)
            inner.append((hidden, grad_gate, grad_up))
        for n in range(0, 2048, STEP):
            cut = slice(n, n + STEP)
            out_piece = total([dot(i[0], h[2][:, cut]) for i, h in zip(inner, halves)])
            grad_piece = total(
                [dot(i[1], h[0][:, cut]) + dot(i[2], h[1][:, cut]) for i, h in zip(inner, halves)]
            )
            part[0, first : first + count, :, cut] = out_piece.astype(BF16).reshape(count, CAP, STEP)
            part[1, first : first + count, :, cut] = grad_piece.astype(BF16).reshape(count, CAP, STEP)
        for r in batch:
            if r:
                returning[r].start()
            else:
                back_own.start()
        if step == SWAP_AT:
            swap_teachers()
        if step == TELL_AT:
            tell()

    for copy in (teacher_out, stat_own, back_own):
        copy.wait()
    teacher_copy.wait_send()
    for copy in telling:
        copy.wait()
    for r in FAR:
        for kind in (0, 1):
            out_going[kind, r].wait_send()
        returning[r].wait()


def token_kernel(
    cot_h, ids_h, prob_h, back_h, stu_h, tea_h, lab_h, stat_h,
    lay_h, ing_h, pgr_h, loss_h, lgr_h,
    cot, ids, prob, back, stu, tea, lab, stat, lay, ing, pgr, loss, lgr, in_sem, back_sem, out_sem, row_sem,
):
    grp = lax.axis_index("grp")
    small = [
        pltpu.make_async_copy(src, dst, in_sem.at[i])
        for i, (src, dst) in enumerate(
            (
                (ids_h, ids), (prob_h, prob), (stat_h, stat), (lab_h, lab), (stu_h.at[0], stu), (tea_h, tea),
                (cot_h, cot),
            )
        )
    ]
    cuts = [slice(n, n + STEP) for n in range(0, 2048, STEP)]
    big = [
        pltpu.make_async_copy(back_h.at[:, :, :, cut], back.at[:, :, :, cut], back_sem.at[i])
        for i, cut in enumerate(cuts)
    ]
    for copy in small + big:
        copy.start()
    stores = [
        pltpu.make_async_copy(src, dst, out_sem.at[i])
        for i, (src, dst) in enumerate(((pgr, pgr_h), (loss, loss_h), (lgr, lgr_h.at[0])))
    ]

    small[0].wait()
    small[1].wait()
    hits, chosen, weight = slot_tables(ids, prob, grp // 2)
    weight_t = weight.T
    chosen_t = chosen.T.astype(BF16)
    weight_hi = weight_t.astype(BF16)
    weight_lo = (weight_t - weight_hi.astype(F32)).astype(BF16)
    for copy in small[2:6]:
        copy.wait()
    seen = [stat[k] for k in range(16)]

    def col(k, i):
        return seen[k][:, i : i + 1]

    max_s = functools.reduce(jnp.maximum, [col(k, 0) for k in range(16)])
    max_t = functools.reduce(jnp.maximum, [col(k, 1) for k in range(16)])
    scale_s = [jnp.exp(col(k, 0) - max_s) for k in range(16)]
    scale_t = [jnp.exp(col(k, 1) - max_t) for k in range(16)]
    sum_s = total([col(k, 2) * scale_s[k] for k in range(16)])
    sum_t = total([col(k, 3) * scale_t[k] for k in range(16)])
    cross = total([col(k, 4) * scale_t[k] for k in range(16)])
    label_logit = total([col(k, 5) for k in range(16)])
    lse_s = max_s + jnp.log(sum_s)
    lse_t = max_t + jnp.log(sum_t)
    student = stu[...].astype(F32)
    teacher = tea[...].astype(F32)
    eye, label_hit = logit_views(lab, student.shape[1], grp)
    value = 2.0 * lse_s - label_logit + cross / sum_t - lse_t
    loss[...] = jnp.sum(jnp.where(eye, value, 0.0), axis=0, keepdims=True)
    onehot = jnp.where(label_hit, 1.0, 0.0)
    lgr[...] = (2.0 * jnp.exp(student - lse_s) - onehot - jnp.exp(teacher - lse_t)).astype(BF16)
    stores[1].start()
    stores[2].start()

    small[6].wait()
    inner_product = jnp.zeros((CHIPS * CAP, 128), F32)
    row_stores = []
    for i, cut in enumerate(cuts):
        big[i].wait()
        rows = back[0, :, :, cut].reshape(CHIPS * CAP, STEP)
        lay[:, cut] = (dot(weight_hi, rows) + dot(weight_lo, rows)).astype(BF16)
        ing[:, cut] = dot(chosen_t, back[1, :, :, cut].reshape(CHIPS * CAP, STEP)).astype(BF16)
        for j, (src, dst) in enumerate(((lay, lay_h), (ing, ing_h))):
            copy = pltpu.make_async_copy(src.at[:, cut], dst.at[:, cut], row_sem.at[j, i])
            copy.start()
            row_stores.append(copy)
        inner_product = inner_product + dot_nt(rows, cot[:, cut])
    inner_product = inner_product * chosen
    for k, h in enumerate(hits):
        pgr[k : k + 1, :] = jnp.sum(jnp.where(h, inner_product, 0.0), axis=0, keepdims=True)
    stores[0].start()
    for copy in stores + row_stores:
        copy.wait()


def body(tokens, cotangent, expert_ids, route_prob, w_gate, w_up, w_down, student, stale, labels):
    expert_ids, route_prob = expert_ids.T, route_prob.T
    w_gate, w_up = jnp.swapaxes(w_gate, 1, 2), jnp.swapaxes(w_up, 1, 2)
    width = student.shape[2]
    logits = (8, width)
    blocks = (2, CHIPS, CAP, 2048)
    dma = pltpu.SemaphoreType.DMA
    anywhere = pl.BlockSpec(memory_space=pl.ANY)
    back, stats, teacher = pl.pallas_call(
        expert_kernel,
        name="experts",
        out_shape=(
            jax.ShapeDtypeStruct(blocks, BF16),
            jax.ShapeDtypeStruct((16, 8, 128), F32),
            jax.ShapeDtypeStruct(logits, BF16),
        ),
        in_specs=[anywhere] * 10,
        out_specs=[anywhere] * 3,
        scratch_shapes=[
            pltpu.VMEM(tokens.shape, BF16),
            pltpu.VMEM(tokens.shape, BF16),
            pltpu.VMEM(expert_ids.shape, jnp.int32),
            pltpu.VMEM(route_prob.shape, F32),
            pltpu.VMEM(w_gate.shape[1:], BF16),
            pltpu.VMEM(w_up.shape[1:], BF16),
            pltpu.VMEM(w_down.shape[1:], BF16),
            pltpu.VMEM(logits, BF16),
            pltpu.VMEM((2,) + logits, BF16),
            pltpu.VMEM(labels.shape, jnp.int32),
            pltpu.VMEM((2, 4, CAP, 2048), BF16),
            pltpu.VMEM(blocks, BF16),
            pltpu.VMEM(blocks, BF16),
            pltpu.VMEM((8, 128), F32),
            pltpu.VMEM((2,) + w_gate.shape[1:], BF16),
            pltpu.VMEM(w_down.shape[1:], BF16),
            dma((9,)),
            dma((3,)),
            dma((3,)),
            dma((3,)),
            dma((2, 8)),
            dma((2, 8)),
            dma((8,)),
            dma((8,)),
            dma((16,)),
            dma((16,)),
            dma((2,)),
            dma((2,)),
        ],
        compiler_params=pltpu.CompilerParams(
            collective_id=0, has_side_effects=True, vmem_limit_bytes=56 << 20
        ),
    )(tokens, cotangent, expert_ids, route_prob, w_gate, w_up, w_down, student, stale, labels)
    layer_out, input_grad, prob_grad, loss, logit_grad = pl.pallas_call(
        token_kernel,
        name="tokens",
        out_shape=(
            jax.ShapeDtypeStruct(tokens.shape, BF16),
            jax.ShapeDtypeStruct(tokens.shape, BF16),
            jax.ShapeDtypeStruct(route_prob.shape, F32),
            jax.ShapeDtypeStruct(labels.shape, F32),
            jax.ShapeDtypeStruct(student.shape, BF16),
        ),
        in_specs=[anywhere] * 8,
        out_specs=[anywhere] * 5,
        scratch_shapes=[
            pltpu.VMEM(tokens.shape, BF16),
            pltpu.VMEM(expert_ids.shape, jnp.int32),
            pltpu.VMEM(route_prob.shape, F32),
            pltpu.VMEM(blocks, BF16),
            pltpu.VMEM(logits, BF16),
            pltpu.VMEM(logits, BF16),
            pltpu.VMEM(labels.shape, jnp.int32),
            pltpu.VMEM((16, 8, 128), F32),
            pltpu.VMEM(tokens.shape, BF16),
            pltpu.VMEM(tokens.shape, BF16),
            pltpu.VMEM(route_prob.shape, F32),
            pltpu.VMEM(labels.shape, F32),
            pltpu.VMEM(logits, BF16),
            dma((7,)),
            dma((4,)),
            dma((3,)),
            dma((2, 4)),
        ],
        compiler_params=pltpu.CompilerParams(vmem_limit_bytes=56 << 20),
    )(cotangent, expert_ids, route_prob, back, student, teacher, labels, stats)
    return layer_out, input_grad, prob_grad.T, loss, logit_grad


def solution(mesh):
    rows = P(("peer", "grp"), None)
    vocab = P("peer", None, "grp")
    peer_row = P("peer", None)
    return jax.shard_map(
        body,
        mesh=mesh,
        in_specs=(
            rows, rows, rows, rows, vocab, vocab, P("peer", "grp", None), vocab, vocab, peer_row,
        ),
        out_specs=(rows, rows, rows, peer_row, vocab),
        check_vma=False,
    )
```

```python
import functools

import jax
import jax.numpy as jnp
from jax import lax
from jax.experimental import pallas as pl
from jax.experimental.pallas import tpu as pltpu
from jax.sharding import PartitionSpec as P

MESH = pl.DeviceIdType.MESH
CAP = 32
EXPERTS = 4
NEAR = (0, 3, 4, 7)
MATE = 1
ORDER = tuple(r for near in NEAR for r in (near, near ^ MATE))
SPOT = {r: i for i, r in enumerate(ORDER)}
KINDS = (0, 1)
STEP = 512
F32 = jnp.float32
BF16 = jnp.bfloat16
NT = (((1,), (1,)), ((), ()))


def dot(a, b):
    return jnp.dot(a, b, preferred_element_type=F32)


def dot_nt(a, b):
    return lax.dot_general(a, b, NT, preferred_element_type=F32)


def total(terms):
    return functools.reduce(jnp.add, terms)


def xor(a, bits, width):
    out = a
    for b in range(width):
        if bits >> b & 1:
            out = out + (1 << b) * (1 - 2 * ((a // (1 << b)) % 2))
    return out


def row_experts(chip):
    rows = lax.broadcasted_iota(jnp.int32, (EXPERTS * CAP, 128), 0)
    return total([jnp.where(rows // CAP == j, xor(chip // 2, j, 2), 0) for j in range(EXPERTS)])


def slot_tables(ids, prob, chip):
    rows = lax.broadcasted_iota(jnp.int32, (EXPERTS * CAP, 128), 0)
    row_expert = row_experts(chip)
    hits = [ids[k : k + 1, :] == row_expert for k in range(4)]
    member = total([h.astype(F32) for h in hits])
    earlier = (
        lax.broadcasted_iota(jnp.int32, (128, 128), 0) < lax.broadcasted_iota(jnp.int32, (128, 128), 1)
    )
    position = dot(member.astype(BF16), earlier.astype(F32).astype(BF16))
    chosen = jnp.where((member > 0.0) & (position.astype(jnp.int32) == rows % CAP), 1.0, 0.0)
    weight = total([jnp.where(h, prob[k : k + 1, :], 0.0) for k, h in enumerate(hits)]) * chosen
    return chosen, weight


def logit_views(lab, width, grp):
    eye = lax.broadcasted_iota(jnp.int32, (8, 8), 0) == lax.broadcasted_iota(jnp.int32, (8, 8), 1)
    label = jnp.sum(jnp.where(eye, lab[...].astype(F32), 0.0), axis=1, keepdims=True).astype(jnp.int32)
    vocab = grp * width + lax.broadcasted_iota(jnp.int32, (8, width), 1)
    return eye, vocab == label


def expert_kernel(
    tok_h, cot_h, ids_h, prob_h, wg_h, wu_h, wd_h, stu_h, sta_h, lab_h,
    back_h, table_h, loss_h, lgr_h,
    tok, cot, ids, prob, wg, wu, wd, stu, tea, lab, send, take, own, part, mate, whole, told, heard, table, loss, lgr, twin_w, twin_d,
    in_sem, out_sem, w_send, w_recv, d_send, d_recv, m_send, m_recv, r_send, r_recv, s_send, s_recv, t_send, t_recv,
):
    peer, grp = lax.axis_index("peer"), lax.axis_index("grp")
    n_peer = lax.axis_size("peer")
    chip, core = grp // 2, grp % 2
    twin = (peer, chip * 2 + (1 - core))
    depth = n_peer // 2
    half, z = peer // depth, lax.rem(peer, depth)
    after = (half * depth + lax.rem(z + 1, depth), grp)
    before = (half * depth + lax.rem(z + depth - 1, depth), grp)
    across = ((1 - half) * depth + z, grp)

    def chip_at(r):
        return (peer, xor(chip, r, 3) * 2 + core)

    barrier = pltpu.get_barrier_semaphore()
    partners = (twin,) + tuple(chip_at(r) for r in (MATE,) + NEAR[1:]) + (after, before, across)
    for partner in partners:
        pl.semaphore_signal(barrier, inc=1, device_id=partner, device_id_type=MESH)

    loads = [
        pltpu.make_async_copy(src, dst, in_sem.at[i])
        for i, (src, dst) in enumerate(
            (
                (ids_h, ids), (prob_h, prob), (tok_h, tok), (cot_h, cot), (stu_h.at[0], stu), (lab_h, lab),
                (wg_h.at[0], wg), (wu_h.at[0], wu), (wd_h.at[0], wd),
            )
        )
    ]
    for copy in loads[:4]:
        copy.start()

    def remote(src, dst, s, r, target):
        return pltpu.make_async_remote_copy(
            src_ref=src, dst_ref=dst, send_sem=s, recv_sem=r, device_id=target, device_id_type=MESH
        )

    def block_to(r, kind, source, target):
        return remote(source, take.at[kind, SPOT[r]], d_send.at[kind, r], d_recv.at[kind, r], chip_at(target))

    out_going = {
        (kind, r): block_to(r, kind, send.at[kind, r // 2], r) for r in (MATE,) + NEAR[1:] for kind in KINDS
    }
    handed_on = {
        (kind, r): block_to(r ^ MATE, kind, take.at[kind, SPOT[r]], MATE) for r in NEAR[1:] for kind in KINDS
    }
    partial = {
        (kind, j): remote(
            part.at[kind, j], mate.at[kind, j], m_send.at[kind, j], m_recv.at[kind, j], chip_at(MATE)
        )
        for j in range(EXPERTS)
        for kind in KINDS
    }
    returning = {
        (kind, j): remote(
            whole.at[kind, j], back_h.at[kind, j], r_send.at[kind, j], r_recv.at[kind, j], chip_at(NEAR[j])
        )
        for j in range(1, EXPERTS)
        for kind in KINDS
    }
    swaps = [
        remote(src, dst, w_send.at[i], w_recv.at[i], twin)
        for i, (src, dst) in enumerate(
            ((wg_h.at[0], twin_w.at[0]), (wu_h.at[0], twin_w.at[1]), (wd_h.at[0], twin_d))
        )
    ]
    teacher_copy = remote(sta_h.at[0], tea.at[0], t_send.at[0], t_recv.at[0], after)
    teacher_swap = remote(tea.at[0], tea.at[1], t_send.at[1], t_recv.at[1], across)

    loads[0].wait()
    loads[1].wait()
    chosen, weight = slot_tables(ids, prob, chip)

    gather = chosen.astype(BF16)
    slot_prob = jnp.sum(weight, axis=1, keepdims=True)
    loads[2].wait()
    for n in range(0, 2048, STEP):
        cut = slice(n, n + STEP)
        send[0, :, :, cut] = dot(gather, tok[:, cut]).astype(BF16).reshape(EXPERTS, CAP, STEP)
    pl.semaphore_wait(barrier, len(partners))
    teacher_copy.start()
    for r in (MATE, 3, 4):
        out_going[0, r].start()
    for copy in loads[4:]:
        copy.start()
    loads[3].wait()
    for n in range(0, 2048, STEP):
        cut = slice(n, n + STEP)
        send[1, :, :, cut] = (slot_prob * dot(gather, cot[:, cut])).astype(BF16).reshape(EXPERTS, CAP, STEP)
    for r in (MATE, 3, 4):
        out_going[1, r].start()
    for kind in KINDS:
        out_going[kind, 7].start()
    for copy in swaps:
        copy.start()

    take[:, 0] = send[:, 0]

    def hand_on(r):
        for kind in KINDS:
            out_going[kind, r].wait_recv()
            handed_on[kind, r].start()

    mine = (z == 0).astype(jnp.int32)

    def swap_teachers():
        teacher_copy.wait_recv()

        @pl.when(z == 0)
        def _():
            teacher_swap.start()

    def local_stats():
        loads[4].wait()
        loads[5].wait()

        @pl.when(z == 0)
        def _():
            teacher_swap.wait()

        student = stu[...].astype(F32)
        teacher = tea[mine].astype(F32)
        label_hit = logit_views(lab, student.shape[1], grp)[1]
        top_s = jnp.max(student, axis=1, keepdims=True)
        top_t = jnp.max(teacher, axis=1, keepdims=True)
        exp_t = jnp.exp(teacher - top_t)
        return (
            top_s,
            top_t,
            jnp.sum(jnp.exp(student - top_s), axis=1, keepdims=True),
            jnp.sum(exp_t, axis=1, keepdims=True),
            jnp.sum(exp_t * (teacher - student), axis=1, keepdims=True),
            jnp.sum(jnp.where(label_hit, student, 0.0), axis=1, keepdims=True),
        )

    telling = [
        remote(told.at[i], heard.at[i], s_send.at[i], s_recv.at[i], target)
        for i, target in enumerate((twin, chip_at(MATE), chip_at(3), chip_at(4)))
    ]

    def tell(i, stats):
        lane = lax.broadcasted_iota(jnp.int32, (8, 128), 1)
        told[i] = total([jnp.where(lane == k, v, 0.0) for k, v in enumerate(stats)])
        telling[i].start()

    def join(i, stats):
        telling[i].wait_recv()
        other = [heard[i, :, k : k + 1] for k in range(6)]
        tops = [jnp.maximum(a, b) for a, b in zip(stats[:2], other[:2])]
        scales = [
            (jnp.exp(a - top), jnp.exp(b - top)) for a, b, top in zip(stats[:2], other[:2], tops)
        ]
        sums = [
            stats[k] * scales[m][0] + other[k] * scales[m][1] for k, m in ((2, 0), (3, 1), (4, 1))
        ]
        return (*tops, *sums, stats[5] + other[5])

    def finish_loss(stats):
        top_s, top_t, sum_s, sum_t, cross, label_logit = stats
        lse_s = top_s + jnp.log(sum_s)
        lse_t = top_t + jnp.log(sum_t)
        student = stu[...].astype(F32)
        teacher = tea[mine].astype(F32)
        eye, label_hit = logit_views(lab, student.shape[1], grp)
        value = 2.0 * lse_s - label_logit + cross / sum_t - lse_t
        loss[...] = jnp.sum(jnp.where(eye, value, 0.0), axis=0, keepdims=True)
        onehot = jnp.where(label_hit, 1.0, 0.0)
        lgr[...] = (2.0 * jnp.exp(student - lse_s) - onehot - jnp.exp(teacher - lse_t)).astype(BF16)

    stores = [
        pltpu.make_async_copy(src, dst, out_sem.at[i])
        for i, (src, dst) in enumerate(
            ((whole.at[:, 0], back_h.at[:, 0]), (table, table_h), (loss, loss_h), (lgr, lgr_h.at[0]))
        )
    ]

    hand_on(3)
    hand_on(4)

    for copy in loads[6:]:
        copy.wait()
    for copy in swaps:
        copy.wait()
    halves = ((wg, wu, wd), (twin_w.at[0], twin_w.at[1], twin_d))

    def work(j):
        spots = slice(2 * j, 2 * j + 2)
        x = take[0, spots].reshape(2 * CAP, 2048)
        s = take[1, spots].reshape(2 * CAP, 2048)
        inner = []
        for gate_w, up_w, down_w in halves:
            gate = dot_nt(x, gate_w[...])
            up = dot_nt(x, up_w[...])
            grad = dot_nt(s, down_w[...])
            sig = jax.nn.sigmoid(gate)
            hidden = (gate * sig * up).astype(BF16)
            grad_gate = (grad * up * sig * (1.0 + gate * (1.0 - sig))).astype(BF16)
            grad_up = (grad * gate * sig).astype(BF16)
            inner.append((hidden, grad_gate, grad_up))
        for n in range(0, 2048, STEP):
            cut = slice(n, n + STEP)
            pieces = (
                total([dot(i[0], h[2][:, cut]) for i, h in zip(inner, halves)]),
                total([dot(i[1], h[0][:, cut]) + dot(i[2], h[1][:, cut]) for i, h in zip(inner, halves)]),
            )
            for kind, piece in enumerate(pieces):
                own[kind, j, :, cut] = piece[:CAP]
                part[kind, j, :, cut] = piece[CAP:].astype(BF16)

    def wait_block(r):
        for kind in KINDS:
            (handed_on[kind, r ^ MATE] if (kind, r ^ MATE) in handed_on else out_going[kind, r]).wait_recv()

    wait_block(MATE)
    work(0)
    swap_teachers()
    hand_on(7)
    wait_block(2)
    work(1)
    for kind in KINDS:
        partial[kind, 1].start()
    stats = local_stats()
    tell(0, stats)
    wait_block(5)
    work(2)
    for kind in KINDS:
        partial[kind, 2].start()
    stats = join(0, stats)
    tell(1, stats)
    wait_block(6)
    work(3)
    for j in (3, 0):
        for kind in KINDS:
            partial[kind, j].start()
    weight_t = weight.T
    weight_hi = weight_t.astype(BF16)
    table[0] = weight_hi
    table[1] = (weight_t - weight_hi.astype(F32)).astype(BF16)
    table[2] = chosen.T.astype(BF16)
    table[3] = gather
    stores[1].start()

    def add_up(j):
        for kind in KINDS:
            partial[kind, j].wait_recv()
            whole[kind, j] = (own[kind, j] + mate[kind, j].astype(F32)).astype(BF16)
            if j:
                returning[kind, j].start()

    add_up(1)
    stats = join(1, stats)
    tell(2, stats)
    add_up(2)
    stats = join(2, stats)
    tell(3, stats)
    add_up(3)
    finish_loss(join(3, stats))
    stores[2].start()
    stores[3].start()
    add_up(0)
    stores[0].start()

    teacher_copy.wait_send()
    for copy in telling:
        copy.wait_send()
    for copies in (out_going, handed_on, partial):
        for copy in copies.values():
            copy.wait_send()
    for copy in returning.values():
        copy.wait()
    for copy in stores:
        copy.wait()


def token_kernel(
    cot_h, ids_h, back_h, table_h, losses_h, logits_h,
    lay_h, ing_h, pgr_h, loss_h, lgr_h,
    cot, ids, back, table, loss, lgr, lay, ing, pgr, in_sem, back_sem, out_sem, row_sem,
):
    grp = lax.axis_index("grp")
    cuts = [slice(n, n + STEP) for n in range(0, 2048, STEP)]
    small = [
        pltpu.make_async_copy(src, dst, in_sem.at[i])
        for i, (src, dst) in enumerate(
            ((table_h, table), (ids_h, ids), (losses_h, loss), (logits_h.at[0], lgr))
        )
    ]
    big = [
        (
            pltpu.make_async_copy(back_h.at[:, :, :, cut], back.at[:, :, :, cut], back_sem.at[0, i]),
            pltpu.make_async_copy(cot_h.at[:, cut], cot.at[:, cut], back_sem.at[1, i]),
        )
        for i, cut in enumerate(cuts)
    ]
    handed = [
        pltpu.make_async_copy(src, dst, out_sem.at[i])
        for i, (src, dst) in enumerate(((loss, loss_h), (lgr, lgr_h.at[0])))
    ]
    store = pltpu.make_async_copy(pgr, pgr_h, out_sem.at[2])
    for copy in small[:2]:
        copy.start()
    for pair in big:
        for copy in pair:
            copy.start()
    for copy in small[2:]:
        copy.start()
    for copy in small[:2]:
        copy.wait()
    inner_product = jnp.zeros((EXPERTS * CAP, 128), F32)
    row_stores = []
    for i, cut in enumerate(cuts):
        for copy in big[i]:
            copy.wait()
        rows = back[0, :, :, cut].reshape(EXPERTS * CAP, STEP)
        lay[:, cut] = (dot(table[0], rows) + dot(table[1], rows)).astype(BF16)
        ing[:, cut] = dot(table[2], back[1, :, :, cut].reshape(EXPERTS * CAP, STEP)).astype(BF16)
        for j, (src, dst) in enumerate(((lay, lay_h), (ing, ing_h))):
            copy = pltpu.make_async_copy(src.at[:, cut], dst.at[:, cut], row_sem.at[j, i])
            copy.start()
            row_stores.append(copy)
        inner_product = inner_product + dot_nt(rows, cot[:, cut])
    for arrived, copy in zip(small[2:], handed):
        arrived.wait()
        copy.start()
    inner_product = inner_product * table[3].astype(F32)
    expert = row_experts(grp // 2)
    for k in range(4):
        pgr[k : k + 1, :] = jnp.sum(
            jnp.where(ids[k : k + 1, :] == expert, inner_product, 0.0), axis=0, keepdims=True
        )
    store.start()
    for copy in handed + row_stores + [store]:
        copy.wait()


def body(tokens, cotangent, expert_ids, route_prob, w_gate, w_up, w_down, student, stale, labels):
    expert_ids, route_prob = expert_ids.T, route_prob.T
    w_gate, w_up = jnp.swapaxes(w_gate, 1, 2), jnp.swapaxes(w_up, 1, 2)
    width = student.shape[2]
    logits = (8, width)
    blocks = (2, EXPERTS, CAP, 2048)
    tables = (4, 128, EXPERTS * CAP)
    dma = pltpu.SemaphoreType.DMA
    anywhere = pl.BlockSpec(memory_space=pl.ANY)
    back, table, losses, logit_rows = pl.pallas_call(
        expert_kernel,
        name="experts",
        out_shape=(
            jax.ShapeDtypeStruct(blocks, BF16),
            jax.ShapeDtypeStruct(tables, BF16),
            jax.ShapeDtypeStruct(labels.shape, F32),
            jax.ShapeDtypeStruct(student.shape, BF16),
        ),
        in_specs=[anywhere] * 10,
        out_specs=[anywhere] * 4,
        scratch_shapes=[
            pltpu.VMEM(tokens.shape, BF16),
            pltpu.VMEM(tokens.shape, BF16),
            pltpu.VMEM(expert_ids.shape, jnp.int32),
            pltpu.VMEM(route_prob.shape, F32),
            pltpu.VMEM(w_gate.shape[1:], BF16),
            pltpu.VMEM(w_up.shape[1:], BF16),
            pltpu.VMEM(w_down.shape[1:], BF16),
            pltpu.VMEM(logits, BF16),
            pltpu.VMEM((2,) + logits, BF16),
            pltpu.VMEM(labels.shape, jnp.int32),
            pltpu.VMEM(blocks, BF16),
            pltpu.VMEM((2, 2 * EXPERTS, CAP, 2048), BF16),
            pltpu.VMEM(blocks, F32),
            pltpu.VMEM(blocks, BF16),
            pltpu.VMEM(blocks, BF16),
            pltpu.VMEM(blocks, BF16),
            pltpu.VMEM((4, 8, 128), F32),
            pltpu.VMEM((4, 8, 128), F32),
            pltpu.VMEM(tables, BF16),
            pltpu.VMEM(labels.shape, F32),
            pltpu.VMEM(logits, BF16),
            pltpu.VMEM((2,) + w_gate.shape[1:], BF16),
            pltpu.VMEM(w_down.shape[1:], BF16),
            dma((9,)),
            dma((4,)),
            dma((3,)),
            dma((3,)),
            dma((2, 8)),
            dma((2, 8)),
            dma((2, EXPERTS)),
            dma((2, EXPERTS)),
            dma((2, EXPERTS)),
            dma((2, EXPERTS)),
            dma((4,)),
            dma((4,)),
            dma((2,)),
            dma((2,)),
        ],
        compiler_params=pltpu.CompilerParams(
            collective_id=0, has_side_effects=True, vmem_limit_bytes=56 << 20
        ),
    )(tokens, cotangent, expert_ids, route_prob, w_gate, w_up, w_down, student, stale, labels)
    layer_out, input_grad, prob_grad, loss, logit_grad = pl.pallas_call(
        token_kernel,
        name="tokens",
        out_shape=(
            jax.ShapeDtypeStruct(tokens.shape, BF16),
            jax.ShapeDtypeStruct(tokens.shape, BF16),
            jax.ShapeDtypeStruct(route_prob.shape, F32),
            jax.ShapeDtypeStruct(labels.shape, F32),
            jax.ShapeDtypeStruct(student.shape, BF16),
        ),
        in_specs=[anywhere] * 6,
        out_specs=[anywhere] * 5,
        scratch_shapes=[
            pltpu.VMEM(tokens.shape, BF16),
            pltpu.VMEM(expert_ids.shape, jnp.int32),
            pltpu.VMEM(blocks, BF16),
            pltpu.VMEM(tables, BF16),
            pltpu.VMEM(labels.shape, F32),
            pltpu.VMEM(logits, BF16),
            pltpu.VMEM(tokens.shape, BF16),
            pltpu.VMEM(tokens.shape, BF16),
            pltpu.VMEM(route_prob.shape, F32),
            dma((4,)),
            dma((2, 4)),
            dma((3,)),
            dma((2, 4)),
        ],
        compiler_params=pltpu.CompilerParams(vmem_limit_bytes=56 << 20),
    )(cotangent, expert_ids, back, table, losses, logit_rows)
    return layer_out, input_grad, prob_grad.T, loss, logit_grad


def solution(mesh):
    rows = P(("peer", "grp"), None)
    vocab = P("peer", None, "grp")
    peer_row = P("peer", None)
    return jax.shard_map(
        body,
        mesh=mesh,
        in_specs=(
            rows, rows, rows, rows, vocab, vocab, P("peer", "grp", None), vocab, vocab, peer_row,
        ),
        out_specs=(rows, rows, rows, peer_row, vocab),
        check_vma=False,
    )
```

```python
import functools

import jax
import jax.numpy as jnp
from jax import lax
from jax.experimental import pallas as pl
from jax.experimental.pallas import tpu as pltpu
from jax.sharding import PartitionSpec as P

MESH = pl.DeviceIdType.MESH
CAP = 32
EXPERTS = 4
NEAR = (0, 3, 4, 7)
MATE = 1
ORDER = tuple(r for near in NEAR for r in (near, near ^ MATE))
SPOT = {r: i for i, r in enumerate(ORDER)}
KINDS = (0, 1)
STEP = 512
F32 = jnp.float32
BF16 = jnp.bfloat16
NT = (((1,), (1,)), ((), ()))


def dot(a, b):
    return jnp.dot(a, b, preferred_element_type=F32)


def dot_nt(a, b):
    return lax.dot_general(a, b, NT, preferred_element_type=F32)


def total(terms):
    return functools.reduce(jnp.add, terms)


def xor(a, bits, width):
    out = a
    for b in range(width):
        if bits >> b & 1:
            out = out + (1 << b) * (1 - 2 * ((a // (1 << b)) % 2))
    return out


def row_experts(chip):
    rows = lax.broadcasted_iota(jnp.int32, (EXPERTS * CAP, 128), 0)
    return total([jnp.where(rows // CAP == j, xor(chip // 2, j, 2), 0) for j in range(EXPERTS)])


def slot_tables(ids, prob, chip):
    rows = lax.broadcasted_iota(jnp.int32, (EXPERTS * CAP, 128), 0)
    row_expert = row_experts(chip)
    hits = [ids[k : k + 1, :] == row_expert for k in range(4)]
    member = total([h.astype(F32) for h in hits])
    earlier = (
        lax.broadcasted_iota(jnp.int32, (128, 128), 0) < lax.broadcasted_iota(jnp.int32, (128, 128), 1)
    )
    position = dot(member.astype(BF16), earlier.astype(F32).astype(BF16))
    chosen = jnp.where((member > 0.0) & (position.astype(jnp.int32) == rows % CAP), 1.0, 0.0)
    weight = total([jnp.where(h, prob[k : k + 1, :], 0.0) for k, h in enumerate(hits)]) * chosen
    return chosen, weight


def logit_views(lab, width, grp):
    eye = lax.broadcasted_iota(jnp.int32, (8, 8), 0) == lax.broadcasted_iota(jnp.int32, (8, 8), 1)
    label = jnp.sum(jnp.where(eye, lab[...].astype(F32), 0.0), axis=1, keepdims=True).astype(jnp.int32)
    vocab = grp * width + lax.broadcasted_iota(jnp.int32, (8, width), 1)
    return eye, vocab == label


def expert_kernel(
    tok_h, cot_h, ids_h, prob_h, wg_h, wu_h, wd_h, stu_h, sta_h, lab_h,
    back_h, table_h, loss_h, lgr_h,
    tok, cot, ids, prob, wg, wu, wd, stu, tea, lab, send, take, own, part, mate, whole, told, heard, table, loss, lgr, twin_w, twin_d,
    in_sem, out_sem, w_send, w_recv, d_send, d_recv, m_send, m_recv, r_send, r_recv, s_send, s_recv, t_send, t_recv,
):
    peer, grp = lax.axis_index("peer"), lax.axis_index("grp")
    n_peer = lax.axis_size("peer")
    chip, core = grp // 2, grp % 2
    twin = (peer, chip * 2 + (1 - core))
    depth = n_peer // 2
    half, z = peer // depth, lax.rem(peer, depth)
    after = (half * depth + lax.rem(z + 1, depth), grp)
    before = (half * depth + lax.rem(z + depth - 1, depth), grp)
    across = ((1 - half) * depth + z, grp)

    def chip_at(r):
        return (peer, xor(chip, r, 3) * 2 + core)

    barrier = pltpu.get_barrier_semaphore()
    partners = (twin,) + tuple(chip_at(r) for r in (MATE,) + NEAR[1:]) + (after, before, across)
    for partner in partners:
        pl.semaphore_signal(barrier, inc=1, device_id=partner, device_id_type=MESH)

    loads = [
        pltpu.make_async_copy(src, dst, in_sem.at[i])
        for i, (src, dst) in enumerate(
            (
                (ids_h, ids), (prob_h, prob), (tok_h, tok), (cot_h, cot), (stu_h.at[0], stu), (lab_h, lab),
                (wg_h.at[0], wg), (wu_h.at[0], wu), (wd_h.at[0], wd),
            )
        )
    ]
    for copy in loads[:4]:
        copy.start()

    def remote(src, dst, s, r, target):
        return pltpu.make_async_remote_copy(
            src_ref=src, dst_ref=dst, send_sem=s, recv_sem=r, device_id=target, device_id_type=MESH
        )

    def both_to(r, source, target):
        return remote(source, take.at[:, SPOT[r]], d_send.at[0, r], d_recv.at[0, r], chip_at(target))

    def block_to(r, kind, source, target):
        return remote(source, take.at[kind, SPOT[r]], d_send.at[kind, r], d_recv.at[kind, r], chip_at(target))

    out_going = {
        (kind, r): block_to(r, kind, send.at[kind, r // 2], r) for r in (MATE,) + NEAR[1:] for kind in KINDS
    }
    handed_on = {
        (kind, r): block_to(r ^ MATE, kind, take.at[kind, SPOT[r]], MATE) for r in (3,) for kind in KINDS
    }
    for r in NEAR[2:]:
        handed_on[0, r] = both_to(r ^ MATE, take.at[:, SPOT[r]], MATE)
    partial = {
        (kind, j): remote(
            part.at[kind, j], mate.at[kind, j], m_send.at[kind, j], m_recv.at[kind, j], chip_at(MATE)
        )
        for j in (0, 3)
        for kind in KINDS
    }
    for j in (1, 2):
        partial[0, j] = remote(part.at[:, j], mate.at[:, j], m_send.at[0, j], m_recv.at[0, j], chip_at(MATE))
    returning = {
        (kind, j): remote(
            whole.at[kind, j], back_h.at[kind, j], r_send.at[kind, j], r_recv.at[kind, j], chip_at(NEAR[j])
        )
        for j in range(1, EXPERTS)
        for kind in KINDS
    }
    swaps = [
        remote(src, dst, w_send.at[i], w_recv.at[i], twin)
        for i, (src, dst) in enumerate(
            ((wg_h.at[0], twin_w.at[0]), (wu_h.at[0], twin_w.at[1]), (wd_h.at[0], twin_d))
        )
    ]
    teacher_copy = remote(sta_h.at[0], tea.at[0], t_send.at[0], t_recv.at[0], after)
    teacher_swap = remote(tea.at[0], tea.at[1], t_send.at[1], t_recv.at[1], across)

    loads[0].wait()
    loads[1].wait()
    chosen, weight = slot_tables(ids, prob, chip)

    gather = chosen.astype(BF16)
    slot_prob = jnp.sum(weight, axis=1, keepdims=True)
    loads[2].wait()
    for n in range(0, 2048, STEP):
        cut = slice(n, n + STEP)
        send[0, :, :, cut] = dot(gather, tok[:, cut]).astype(BF16).reshape(EXPERTS, CAP, STEP)
    pl.semaphore_wait(barrier, len(partners))
    teacher_copy.start()
    for r in (MATE, 3, 4):
        out_going[0, r].start()
    for copy in loads[4:]:
        copy.start()
    loads[3].wait()
    for n in range(0, 2048, STEP):
        cut = slice(n, n + STEP)
        send[1, :, :, cut] = (slot_prob * dot(gather, cot[:, cut])).astype(BF16).reshape(EXPERTS, CAP, STEP)
    for r in (MATE, 3, 4):
        out_going[1, r].start()
    for kind in KINDS:
        out_going[kind, 7].start()
    for copy in swaps:
        copy.start()

    take[:, 0] = send[:, 0]

    def hand_on(r):
        for kind in KINDS:
            out_going[kind, r].wait_recv()
            if (1, r) in handed_on:
                handed_on[kind, r].start()
        if (1, r) not in handed_on:
            handed_on[0, r].start()

    mine = (z == 0).astype(jnp.int32)

    def swap_teachers():
        teacher_copy.wait_recv()

        @pl.when(z == 0)
        def _():
            teacher_swap.start()

    def local_stats():
        loads[4].wait()
        loads[5].wait()

        @pl.when(z == 0)
        def _():
            teacher_swap.wait()

        student = stu[...].astype(F32)
        teacher = tea[mine].astype(F32)
        label_hit = logit_views(lab, student.shape[1], grp)[1]
        top_s = jnp.max(student, axis=1, keepdims=True)
        top_t = jnp.max(teacher, axis=1, keepdims=True)
        exp_t = jnp.exp(teacher - top_t)
        return (
            top_s,
            top_t,
            jnp.sum(jnp.exp(student - top_s), axis=1, keepdims=True),
            jnp.sum(exp_t, axis=1, keepdims=True),
            jnp.sum(exp_t * (teacher - student), axis=1, keepdims=True),
            jnp.sum(jnp.where(label_hit, student, 0.0), axis=1, keepdims=True),
        )

    telling = [
        remote(told.at[i], heard.at[i], s_send.at[i], s_recv.at[i], target)
        for i, target in enumerate((twin, chip_at(MATE), chip_at(3), chip_at(4)))
    ]

    def tell(i, stats):
        lane = lax.broadcasted_iota(jnp.int32, (8, 128), 1)
        told[i] = total([jnp.where(lane == k, v, 0.0) for k, v in enumerate(stats)])
        telling[i].start()

    def join(i, stats):
        telling[i].wait_recv()
        other = [heard[i, :, k : k + 1] for k in range(6)]
        tops = [jnp.maximum(a, b) for a, b in zip(stats[:2], other[:2])]
        scales = [
            (jnp.exp(a - top), jnp.exp(b - top)) for a, b, top in zip(stats[:2], other[:2], tops)
        ]
        sums = [
            stats[k] * scales[m][0] + other[k] * scales[m][1] for k, m in ((2, 0), (3, 1), (4, 1))
        ]
        return (*tops, *sums, stats[5] + other[5])

    def finish_loss(stats):
        top_s, top_t, sum_s, sum_t, cross, label_logit = stats
        lse_s = top_s + jnp.log(sum_s)
        lse_t = top_t + jnp.log(sum_t)
        student = stu[...].astype(F32)
        teacher = tea[mine].astype(F32)
        eye, label_hit = logit_views(lab, student.shape[1], grp)
        value = 2.0 * lse_s - label_logit + cross / sum_t - lse_t
        loss[...] = jnp.sum(jnp.where(eye, value, 0.0), axis=0, keepdims=True)
        onehot = jnp.where(label_hit, 1.0, 0.0)
        lgr[...] = (2.0 * jnp.exp(student - lse_s) - onehot - jnp.exp(teacher - lse_t)).astype(BF16)

    stores = [
        pltpu.make_async_copy(src, dst, out_sem.at[i])
        for i, (src, dst) in enumerate(
            (
                (whole.at[0, 0], back_h.at[0, 0]), (table, table_h), (loss, loss_h), (lgr, lgr_h.at[0]),
                (whole.at[1, 0], back_h.at[1, 0]),
            )
        )
    ]

    hand_on(3)
    hand_on(4)

    for copy in loads[6:]:
        copy.wait()
    for copy in swaps:
        copy.wait()
    halves = ((wg, wu, wd), (twin_w.at[0], twin_w.at[1], twin_d))

    def work(j):
        spots = slice(2 * j, 2 * j + 2)
        x = take[0, spots].reshape(2 * CAP, 2048)
        s = take[1, spots].reshape(2 * CAP, 2048)
        inner = []
        for gate_w, up_w, down_w in halves:
            gate = dot_nt(x, gate_w[...])
            up = dot_nt(x, up_w[...])
            grad = dot_nt(s, down_w[...])
            sig = jax.nn.sigmoid(gate)
            hidden = (gate * sig * up).astype(BF16)
            grad_gate = (grad * up * sig * (1.0 + gate * (1.0 - sig))).astype(BF16)
            grad_up = (grad * gate * sig).astype(BF16)
            inner.append((hidden, grad_gate, grad_up))
        for n in range(0, 2048, STEP):
            cut = slice(n, n + STEP)
            pieces = (
                total([dot(i[0], h[2][:, cut]) for i, h in zip(inner, halves)]),
                total([dot(i[1], h[0][:, cut]) + dot(i[2], h[1][:, cut]) for i, h in zip(inner, halves)]),
            )
            for kind, piece in enumerate(pieces):
                own[kind, j, :, cut] = piece[:CAP]
                part[kind, j, :, cut] = piece[CAP:].astype(BF16)

    def wait_block(r):
        for copies, key in ((handed_on, r ^ MATE), (out_going, r)):
            for kind in KINDS:
                if (kind, key) in copies:
                    copies[kind, key].wait_recv()

    wait_block(MATE)
    work(0)
    swap_teachers()
    hand_on(7)
    wait_block(2)
    work(1)
    partial[0, 1].start()
    stats = local_stats()
    tell(0, stats)
    wait_block(5)
    work(2)
    partial[0, 2].start()
    stats = join(0, stats)
    tell(1, stats)
    wait_block(6)
    work(3)
    for j in (3, 0):
        for kind in KINDS:
            partial[kind, j].start()
    weight_t = weight.T
    weight_hi = weight_t.astype(BF16)
    table[0] = weight_hi
    table[1] = (weight_t - weight_hi.astype(F32)).astype(BF16)
    table[2] = chosen.T.astype(BF16)
    table[3] = gather
    stores[1].start()

    def add_up(j):
        for kind in KINDS:
            if (kind, j) in partial:
                partial[kind, j].wait_recv()
            whole[kind, j] = (own[kind, j] + mate[kind, j].astype(F32)).astype(BF16)
            if j:
                returning[kind, j].start()
            else:
                stores[4 * kind].start()

    add_up(1)
    stats = join(1, stats)
    tell(2, stats)
    add_up(2)
    stats = join(2, stats)
    tell(3, stats)
    add_up(3)
    finish_loss(join(3, stats))
    stores[2].start()
    stores[3].start()
    add_up(0)

    teacher_copy.wait_send()
    for copy in telling:
        copy.wait_send()
    for copies in (out_going, handed_on, partial):
        for copy in copies.values():
            copy.wait_send()
    for copy in returning.values():
        copy.wait()
    for copy in stores:
        copy.wait()


def token_kernel(
    cot_h, ids_h, back_h, table_h, losses_h, logits_h,
    lay_h, ing_h, pgr_h, loss_h, lgr_h,
    cot, ids, back, table, loss, lgr, lay, ing, pgr, in_sem, back_sem, out_sem, row_sem,
):
    grp = lax.axis_index("grp")
    cuts = [slice(n, n + STEP) for n in range(0, 2048, STEP)]
    small = [
        pltpu.make_async_copy(src, dst, in_sem.at[i])
        for i, (src, dst) in enumerate(
            ((table_h, table), (ids_h, ids), (losses_h, loss), (logits_h.at[0], lgr))
        )
    ]
    big = [
        (
            pltpu.make_async_copy(back_h.at[:, :, :, cut], back.at[:, :, :, cut], back_sem.at[0, i]),
            pltpu.make_async_copy(cot_h.at[:, cut], cot.at[:, cut], back_sem.at[1, i]),
        )
        for i, cut in enumerate(cuts)
    ]
    handed = [
        pltpu.make_async_copy(src, dst, out_sem.at[i])
        for i, (src, dst) in enumerate(((loss, loss_h), (lgr, lgr_h.at[0])))
    ]
    store = pltpu.make_async_copy(pgr, pgr_h, out_sem.at[2])
    for copy in small[:2]:
        copy.start()
    for pair in big:
        for copy in pair:
            copy.start()
    for copy in small[2:]:
        copy.start()
    for copy in small[:2]:
        copy.wait()

    def share_out(inner_product):
        inner_product = inner_product * table[3].astype(F32)
        expert = row_experts(grp // 2)
        for k in range(4):
            pgr[k : k + 1, :] = jnp.sum(
                jnp.where(ids[k : k + 1, :] == expert, inner_product, 0.0), axis=0, keepdims=True
            )
        store.start()

    inner_product = jnp.zeros((EXPERTS * CAP, 128), F32)
    row_stores = []
    for i, cut in enumerate(cuts):
        for copy in big[i]:
            copy.wait()
        rows = back[0, :, :, cut].reshape(EXPERTS * CAP, STEP)
        inner_product = inner_product + dot_nt(rows, cot[:, cut])
        if i == len(cuts) - 1:
            share_out(inner_product)
        lay[:, cut] = (dot(table[0], rows) + dot(table[1], rows)).astype(BF16)
        ing[:, cut] = dot(table[2], back[1, :, :, cut].reshape(EXPERTS * CAP, STEP)).astype(BF16)
        for j, (src, dst) in enumerate(((lay, lay_h), (ing, ing_h))):
            copy = pltpu.make_async_copy(src.at[:, cut], dst.at[:, cut], row_sem.at[j, i])
            copy.start()
            row_stores.append(copy)
    for arrived, copy in zip(small[2:], handed):
        arrived.wait()
        copy.start()
    for copy in handed + row_stores + [store]:
        copy.wait()


def body(tokens, cotangent, expert_ids, route_prob, w_gate, w_up, w_down, student, stale, labels):
    expert_ids, route_prob = expert_ids.T, route_prob.T
    w_gate, w_up = jnp.swapaxes(w_gate, 1, 2), jnp.swapaxes(w_up, 1, 2)
    width = student.shape[2]
    logits = (8, width)
    blocks = (2, EXPERTS, CAP, 2048)
    tables = (4, 128, EXPERTS * CAP)
    dma = pltpu.SemaphoreType.DMA
    anywhere = pl.BlockSpec(memory_space=pl.ANY)
    back, table, losses, logit_rows = pl.pallas_call(
        expert_kernel,
        name="experts",
        out_shape=(
            jax.ShapeDtypeStruct(blocks, BF16),
            jax.ShapeDtypeStruct(tables, BF16),
            jax.ShapeDtypeStruct(labels.shape, F32),
            jax.ShapeDtypeStruct(student.shape, BF16),
        ),
        in_specs=[anywhere] * 10,
        out_specs=[anywhere] * 4,
        scratch_shapes=[
            pltpu.VMEM(tokens.shape, BF16),
            pltpu.VMEM(tokens.shape, BF16),
            pltpu.VMEM(expert_ids.shape, jnp.int32),
            pltpu.VMEM(route_prob.shape, F32),
            pltpu.VMEM(w_gate.shape[1:], BF16),
            pltpu.VMEM(w_up.shape[1:], BF16),
            pltpu.VMEM(w_down.shape[1:], BF16),
            pltpu.VMEM(logits, BF16),
            pltpu.VMEM((2,) + logits, BF16),
            pltpu.VMEM(labels.shape, jnp.int32),
            pltpu.VMEM(blocks, BF16),
            pltpu.VMEM((2, 2 * EXPERTS, CAP, 2048), BF16),
            pltpu.VMEM(blocks, F32),
            pltpu.VMEM(blocks, BF16),
            pltpu.VMEM(blocks, BF16),
            pltpu.VMEM(blocks, BF16),
            pltpu.VMEM((4, 8, 128), F32),
            pltpu.VMEM((4, 8, 128), F32),
            pltpu.VMEM(tables, BF16),
            pltpu.VMEM(labels.shape, F32),
            pltpu.VMEM(logits, BF16),
            pltpu.VMEM((2,) + w_gate.shape[1:], BF16),
            pltpu.VMEM(w_down.shape[1:], BF16),
            dma((9,)),
            dma((5,)),
            dma((3,)),
            dma((3,)),
            dma((2, 8)),
            dma((2, 8)),
            dma((2, EXPERTS)),
            dma((2, EXPERTS)),
            dma((2, EXPERTS)),
            dma((2, EXPERTS)),
            dma((4,)),
            dma((4,)),
            dma((2,)),
            dma((2,)),
        ],
        compiler_params=pltpu.CompilerParams(
            collective_id=0, has_side_effects=True, vmem_limit_bytes=56 << 20
        ),
    )(tokens, cotangent, expert_ids, route_prob, w_gate, w_up, w_down, student, stale, labels)
    layer_out, input_grad, prob_grad, loss, logit_grad = pl.pallas_call(
        token_kernel,
        name="tokens",
        out_shape=(
            jax.ShapeDtypeStruct(tokens.shape, BF16),
            jax.ShapeDtypeStruct(tokens.shape, BF16),
            jax.ShapeDtypeStruct(route_prob.shape, F32),
            jax.ShapeDtypeStruct(labels.shape, F32),
            jax.ShapeDtypeStruct(student.shape, BF16),
        ),
        in_specs=[anywhere] * 6,
        out_specs=[anywhere] * 5,
        scratch_shapes=[
            pltpu.VMEM(tokens.shape, BF16),
            pltpu.VMEM(expert_ids.shape, jnp.int32),
            pltpu.VMEM(blocks, BF16),
            pltpu.VMEM(tables, BF16),
            pltpu.VMEM(labels.shape, F32),
            pltpu.VMEM(logits, BF16),
            pltpu.VMEM(tokens.shape, BF16),
            pltpu.VMEM(tokens.shape, BF16),
            pltpu.VMEM(route_prob.shape, F32),
            dma((4,)),
            dma((2, 4)),
            dma((3,)),
            dma((2, 4)),
        ],
        compiler_params=pltpu.CompilerParams(vmem_limit_bytes=56 << 20),
    )(cotangent, expert_ids, back, table, losses, logit_rows)
    return layer_out, input_grad, prob_grad.T, loss, logit_grad


def solution(mesh):
    rows = P(("peer", "grp"), None)
    vocab = P("peer", None, "grp")
    peer_row = P("peer", None)
    return jax.shard_map(
        body,
        mesh=mesh,
        in_specs=(
            rows, rows, rows, rows, vocab, vocab, P("peer", "grp", None), vocab, vocab, peer_row,
        ),
        out_specs=(rows, rows, rows, peer_row, vocab),
        check_vma=False,
    )
```
